32 devices in a mesh: groups: 2 (over y), latent: 4 (over z), width: 4 (over x, core).
Axes of the slice: x: 2, y: 2, z: 4, core: 2. Of those that a mesh axis runs over, the one named last changes fastest.
Arguments:
- acts: bfloat16 [512, 5120], P(('groups', 'latent'), 'width'), parts along dimension 0, may hold values from -6 to 6
- dec_bias: float32 [10240], P(('groups', 'width')), parts along dimension 0, may hold values from -3 to 3
- enc_weight: bfloat16 [5120, 1024], P('width', ('groups', 'latent')), parts along dimension 1, may hold values from -0.078125 to 0.078125
- enc_bias: float32 [1024], P(('groups', 'latent')), parts along dimension 0, may hold values from -3 to 3
- dec_weight: bfloat16 [1024, 5120], P(('groups', 'latent'), 'width'), parts along dimension 0, may hold values from -0.25 to 0.25
- enc_m: float32 [5120, 1024], P('width', ('groups', 'latent')), parts along dimension 1, may hold values from -0.6 to 0.6
- enc_v: float32 [5120, 1024], P('width', ('groups', 'latent')), parts along dimension 1, may hold values from 0.0001 to 0.01
- dec_m: float32 [1024, 5120], P(('groups', 'latent'), 'width'), parts along dimension 0, may hold values from -0.6 to 0.6
- dec_v: float32 [1024, 5120], P(('groups', 'latent'), 'width'), parts along dimension 0, may hold values from 0.0001 to 0.01
- bias_m: float32 [1024], P(('groups', 'latent')), parts along dimension 0, may hold values from -0.6 to 0.6
- bias_v: float32 [1024], P(('groups', 'latent')), parts along dimension 0, may hold values from 0.0001 to 0.01
Outputs:
- enc_moment: float32 [5120, 1024], P('width', ('groups', 'latent')), parts along dimension 1
- enc_second: float32 [5120, 1024], P('width', ('groups', 'latent')), parts along dimension 1
- enc_step: bfloat16 [5120, 1024], P('width', ('groups', 'latent')), parts along dimension 1
- dec_moment: float32 [1024, 5120], P(('groups', 'latent'), 'width'), parts along dimension 0
- dec_second: float32 [1024, 5120], P(('groups', 'latent'), 'width'), parts along dimension 0
- dec_step: bfloat16 [1024, 5120], P(('groups', 'latent'), 'width'), parts along dimension 0
- bias_moment: float32 [1024], P(('groups', 'latent')), parts along dimension 0
- bias_second: float32 [1024], P(('groups', 'latent')), parts along dimension 0
- bias_step: bfloat16 [1024], P(('groups', 'latent')), parts along dimension 0
The draws below stay inside these ranges and needn't reach their ends.
There are 2 independent parts, one for each index of `groups`. The reference program is written for one: setup_inputs(seed, part) draws one part's arguments, and reference() takes and returns one part's arrays. A program takes and returns all parts, laid end to end along the dimension named above; each array names one. Nothing has to cross between parts.
All inputs are finite; a program needn't handle non-finite values.
Results may differ from the reference program's by a relative error of at most 0.006.
The reference program's roundings to bfloat16 on the way (of `centered`, `latent_code`, `grad_out` and `pre_grad`) count: a program that leaves them out, or rounds other values in their place, can miss the bound.
Values may be sent and summed in bfloat16 or wider, within the bound.
A program may use at most 64 MiB of HBM per device.

```python
import math
import jax
import jax.numpy as jnp
from jax import lax

D = 5120
ADAM_STEP = 10
LATENTS = 512
ROWS = 256


def block_scale(key, shape, shards, low, largest):
    factor_of = 1.0
    for position, blocks in shards:
        steps = jax.random.uniform(jax.random.fold_in(jax.random.fold_in(key, 6), position), (blocks,), jnp.float32, low / len(shards), largest / len(shards))
        factor_of = factor_of * jnp.repeat(jnp.exp(steps), shape[position] // blocks).reshape((-1,) + (1,) * (len(shape) - 1 - position))
    return factor_of


def normal_values(stream_key, extent, width, reach, shards=(), kind=jnp.bfloat16):
    factor_of = block_scale(stream_key, extent, shards, -0.22, 0.18) if shards else 1.0
    entries = jax.random.normal(stream_key, extent, jnp.float32) * width * factor_of
    return jnp.minimum(jnp.maximum(entries, -reach), reach).astype(kind)


def setup_inputs(seed: int = 0, part: int = 0) -> dict:
    arg_keys = jax.random.split(jax.random.key(seed), 12)
    part_keys = jax.random.split(jax.random.fold_in(arg_keys[11], part), 12)
    return {
        "acts": normal_values(part_keys[0], (ROWS, D), 1.0, 6.0, ((0, 4), (1, 4))),
        "dec_bias": normal_values(part_keys[1], (D,), 0.5, 3.0, ((0, 4),), jnp.float32),
        "enc_weight": normal_values(part_keys[2], (D, LATENTS), D ** -0.5, 0.078125, ((0, 4), (1, 4))),
        "enc_bias": normal_values(part_keys[3], (LATENTS,), 0.5, 3.0, ((0, 4),), jnp.float32),
        "dec_weight": normal_values(part_keys[4], (LATENTS, D), LATENTS ** -0.5, 0.25, ((0, 4), (1, 4))),
        "enc_m": normal_values(part_keys[5], (D, LATENTS), 0.1, 0.6, ((0, 4), (1, 4)), jnp.float32),
        "enc_v": jnp.clip(jnp.exp(math.log(0.01) - 4.6051702 * jax.random.uniform(part_keys[6], (D, LATENTS), jnp.float32) ** block_scale(part_keys[6], (D, LATENTS), ((0, 4), (1, 4)), -0.2, 0.2)), 0.0001, 0.01),
        "dec_m": normal_values(part_keys[7], (LATENTS, D), 0.1, 0.6, ((0, 4), (1, 4)), jnp.float32),
        "dec_v": jnp.clip(jnp.exp(math.log(0.01) - 4.6051702 * jax.random.uniform(part_keys[8], (LATENTS, D), jnp.float32) ** block_scale(part_keys[8], (LATENTS, D), ((0, 4), (1, 4)), -0.2, 0.2)), 0.0001, 0.01),
        "bias_m": normal_values(part_keys[9], (LATENTS,), 0.1, 0.6, ((0, 4),), jnp.float32),
        "bias_v": jnp.clip(jnp.exp(math.log(0.01) - 4.6051702 * jax.random.uniform(part_keys[10], (LATENTS,), jnp.float32) ** block_scale(part_keys[10], (LATENTS,), ((0, 4),), -0.2, 0.2)), 0.0001, 0.01),
    }


BETA_ONE = 0.9
BETA_TWO = 0.95
EPSILON = 1e-08
SPARSITY = 0.5
SHARPNESS = 4.0

def adam_update(moment, second, grad):
    moment_new = BETA_ONE * moment + (1.0 - BETA_ONE) * grad
    second_new = BETA_TWO * second + (1.0 - BETA_TWO) * grad * grad
    update_step = moment_new / (1.0 - BETA_ONE ** ADAM_STEP) / (jnp.sqrt(second_new / (1.0 - BETA_TWO ** ADAM_STEP)) + EPSILON)
    return (moment_new, second_new, update_step.astype(jnp.bfloat16))

def reference(acts, dec_bias, enc_weight, enc_bias, dec_weight, enc_m, enc_v, dec_m, dec_v, bias_m, bias_v):
    centered = (acts.astype(jnp.float32) - dec_bias).astype(jnp.bfloat16)
    pre = jnp.dot(centered, enc_weight, preferred_element_type=jnp.float32) + enc_bias
    rectified = jax.nn.softplus(SHARPNESS * pre) / SHARPNESS
    latent_code = rectified.astype(jnp.bfloat16)
    rebuilt = jnp.dot(latent_code, dec_weight, preferred_element_type=jnp.float32) + dec_bias
    grad_out = (2.0 / ROWS * (rebuilt - acts.astype(jnp.float32))).astype(jnp.bfloat16)
    dec_grad = jnp.dot(latent_code.T, grad_out, preferred_element_type=jnp.float32)
    code_grad = jnp.dot(grad_out, dec_weight.T, preferred_element_type=jnp.float32) + SPARSITY / ROWS
    pre_grad = (code_grad * jax.nn.sigmoid(SHARPNESS * pre)).astype(jnp.bfloat16)
    enc_grad = jnp.dot(centered.T, pre_grad, preferred_element_type=jnp.float32)
    bias_grad = lax.optimization_barrier(jnp.sum(pre_grad.astype(jnp.float32), axis=0))
    enc_moment, enc_second, enc_step = adam_update(enc_m, enc_v, enc_grad)
    dec_moment, dec_second, dec_step = adam_update(dec_m, dec_v, dec_grad)
    bias_moment, bias_second, bias_step = adam_update(bias_m, bias_v, bias_grad)
    return (enc_moment, enc_second, enc_step, dec_moment, dec_second, dec_step, bias_moment, bias_second, bias_step)
```

```python
import functools

import jax
import jax.numpy as jnp
from jax import lax
from jax.experimental import pallas as pl
from jax.experimental.pallas import tpu as pltpu
from jax.sharding import PartitionSpec as P

ADAM_STEP = 10


BETA_ONE = 0.9
BETA_TWO = 0.95
EPSILON = 1e-08
SPARSITY = 0.5
SHARPNESS = 4.0

MESH = pl.DeviceIdType.MESH


def adam_update(moment, second, grad):
    moment_new = BETA_ONE * moment + (1.0 - BETA_ONE) * grad
    second_new = BETA_TWO * second + (1.0 - BETA_TWO) * grad * grad
    update_step = (
        moment_new
        / (1.0 - BETA_ONE**ADAM_STEP)
        / (jnp.sqrt(second_new / (1.0 - BETA_TWO**ADAM_STEP)) + EPSILON)
    )
    return (moment_new, second_new, update_step.astype(jnp.bfloat16))


def inner_rows(left, right):
    return lax.dot_general(
        left, right, (((0,), (0,)), ((), ())), preferred_element_type=jnp.float32
    )


def inner_cols(left, right):
    return lax.dot_general(
        left, right, (((1,), (1,)), ((), ())), preferred_element_type=jnp.float32
    )


def local_large(
    acts, dec_bias, enc_weight, enc_bias, dec_weight, enc_m, enc_v, dec_m, dec_v, bias_m, bias_v
):
    lat_groups = lax.axis_size("latent")
    rows_local = acts.shape[0]
    rows_all = rows_local * lat_groups
    incoming = lax.all_gather(acts, "latent", axis=0, tiled=True)
    centered_block = (incoming.astype(jnp.float32) - dec_bias).astype(jnp.bfloat16)
    product = jnp.dot(centered_block, enc_weight, preferred_element_type=jnp.float32)
    pre_part = product
    raw_rows = incoming
    centered = centered_block
    pre_part, raw_rows, centered = (pre_part, raw_rows, centered)
    pre = lax.psum(pre_part, "width") + enc_bias
    latent_code = (jax.nn.softplus(SHARPNESS * pre) / SHARPNESS).astype(jnp.bfloat16)
    codes = latent_code
    rebuilt = (
        lax.psum_scatter(
            jnp.dot(codes, dec_weight, preferred_element_type=jnp.float32),
            "latent",
            scatter_dimension=0,
            tiled=True,
        )
        + dec_bias
    )
    grad_out = (2.0 / rows_all * (rebuilt - acts.astype(jnp.float32))).astype(jnp.bfloat16)
    incoming = lax.all_gather(grad_out, "latent", axis=0, tiled=True)
    codes = latent_code
    dec_grad = inner_rows(codes, incoming)
    code_part = inner_cols(incoming, dec_weight)
    dec_grad, code_part = (dec_grad, code_part)
    code_grad = lax.psum(code_part, "width") + SPARSITY / rows_all
    pre_grad = (code_grad * jax.nn.sigmoid(SHARPNESS * pre)).astype(jnp.bfloat16)
    enc_grad = inner_rows(centered, pre_grad)
    bias_grad = jnp.sum(pre_grad.astype(jnp.float32), axis=0)
    enc_moment, enc_second, enc_step = adam_update(enc_m, enc_v, enc_grad)
    dec_moment, dec_second, dec_step = adam_update(dec_m, dec_v, dec_grad)
    bias_moment, bias_second, bias_step = adam_update(bias_m, bias_v, bias_grad)
    return (
        enc_moment,
        enc_second,
        enc_step,
        dec_moment,
        dec_second,
        dec_step,
        bias_moment,
        bias_second,
        bias_step,
    )


def exchange_kernel(
    n,
    nw,
    acts_ref,
    dec_bias_ref,
    enc_weight_ref,
    enc_bias_ref,
    dec_weight_ref,
    centered,
    codes,
    grad_out,
    pre_grad,
    acts_all,
    pre_parts,
    code_parts,
    slope,
    product,
    total,
    left_sum,
    right_sum,
    to_right,
    to_left,
    acts_recv,
    acts_send_right,
    acts_send_left,
    left_recv,
    right_recv,
    right_send,
    left_send,
    pre_recv,
    pre_send,
    code_recv,
    code_send,
):
    place = lax.axis_index("latent")
    mine = lax.axis_index("width")
    rows_all = n * acts_ref.shape[0]
    peers = [lax.rem(mine + k, nw) for k in range(1, nw)]

    barrier = pltpu.get_barrier_semaphore()
    for peer in peers:
        pl.semaphore_signal(barrier, inc=1, device_id={"width": peer}, device_id_type=MESH)

    @pl.when(place > 0)
    def _():
        pl.semaphore_signal(barrier, inc=1, device_id={"latent": place - 1}, device_id_type=MESH)

    @pl.when(place < n - 1)
    def _():
        pl.semaphore_signal(barrier, inc=1, device_id={"latent": place + 1}, device_id_type=MESH)

    pl.semaphore_wait(
        barrier, nw - 1 + jnp.where(place > 0, 1, 0) + jnp.where(place < n - 1, 1, 0)
    )

    def program(z):
        sent = []
        right = {"latent": place + 1}
        left = {"latent": place - 1}
        some = right if z < n - 1 else left

        def acts_block(b):
            return acts_ref if b == z else acts_all.at[b]

        def copy(src, dst, send, recv, where):
            return pltpu.make_async_remote_copy(
                src_ref=src,
                dst_ref=dst,
                send_sem=send,
                recv_sem=recv,
                device_id=where,
                device_id_type=MESH,
            )

        def send(*arguments):
            descriptor = copy(*arguments)
            descriptor.start()
            sent.append(descriptor)

        def acts_right(b):
            send(acts_block(b), acts_all.at[b], acts_send_right.at[b], acts_recv.at[b], right)

        def acts_left(b):
            send(acts_block(b), acts_all.at[b], acts_send_left.at[b], acts_recv.at[b], left)

        def to_peers(parts, b, send_sem, recv_sem):
            for k in range(1, nw):
                block = parts.at[mine, b]
                send(block, block, send_sem.at[k, b], recv_sem.at[k, b], {"width": peers[k - 1]})

        def from_peers(parts, b, send_sem, recv_sem):
            for k in range(1, nw):
                block = parts.at[mine, b]
                copy(
                    block, block, send_sem.at[k, b], recv_sem.at[k, b], {"width": peers[k - 1]}
                ).wait_recv()
            total = parts[0, b]
            for other in range(1, nw):
                total = total + parts[other, b]
            return total

        def start_pre(b):
            rounded = (acts_block(b)[...].astype(jnp.float32) - dec_bias_ref[...]).astype(
                jnp.bfloat16
            )
            centered[b] = rounded
            pre_parts[mine, b] = jnp.dot(
                rounded, enc_weight_ref[...], preferred_element_type=jnp.float32
            )
            to_peers(pre_parts, b, pre_send, pre_recv)

        def finish_pre(b):
            scaled = SHARPNESS * (from_peers(pre_parts, b, pre_send, pre_recv) + enc_bias_ref[...])
            small = jnp.exp(-jnp.abs(scaled))
            code = ((jnp.maximum(scaled, 0.0) + jnp.log1p(small)) / SHARPNESS).astype(jnp.bfloat16)
            slope[b] = jnp.where(scaled >= 0, 1.0, small) / (1.0 + small)
            codes[b] = code
            own = jnp.dot(code, dec_weight_ref[...], preferred_element_type=jnp.float32)
            product[b] = own
            total[b] = own + dec_bias_ref[...]

        def sum_right(i):
            partial = product[i]
            if z > 0:
                arrived = left_sum[i]
                partial = partial + arrived
                total[i] = total[i] + arrived
            if z < n - 1:
                to_right[i] = partial
                send(to_right.at[i], left_sum.at[i], right_send.at[i], left_recv.at[i], right)

        def sum_left(i):
            partial = product[i]
            if z < n - 1:
                arrived = right_sum[i]
                partial = partial + arrived
                total[i] = total[i] + arrived
            if z > 0:
                to_left[i] = partial
                send(to_left.at[i], right_sum.at[i], left_send.at[i], right_recv.at[i], left)

        def start_code(i):
            rounded = (2.0 / rows_all * (total[i] - acts_block(i)[...].astype(jnp.float32))).astype(
                jnp.bfloat16
            )
            grad_out[i] = rounded
            code_parts[mine, i] = inner_cols(rounded, dec_weight_ref[...])
            to_peers(code_parts, i, code_send, code_recv)

        def finish_code(i):
            code_grad = from_peers(code_parts, i, code_send, code_recv) + SPARSITY / rows_all
            pre_grad[i] = (code_grad * slope[i]).astype(jnp.bfloat16)

        if z < n - 1:
            acts_right(z)
        if z > 0:
            acts_left(z)
        start_pre(z)
        waiting_pre, waiting_code = [z], []
        for step in range(1, 2 * n):
            for b in waiting_pre:
                finish_pre(b)
                if z == 0:
                    sum_right(b)
                if z == n - 1:
                    sum_left(b)
            for i in waiting_code:
                finish_code(i)
            waiting_pre, waiting_code = [], []
            for b, onward in ((z - step, acts_right), (z + step, acts_left)):
                if 0 <= b < n:
                    copy(
                        acts_all.at[b],
                        acts_all.at[b],
                        acts_send_right.at[b],
                        acts_recv.at[b],
                        some,
                    ).wait_recv()
                    if (onward is acts_right and z < n - 1) or (onward is acts_left and z > 0):
                        onward(b)
                    waiting_pre.append(b)
            for b in waiting_pre:
                start_pre(b)
            i = step - 1 - z
            if z > 0 and 0 <= i < n:
                copy(
                    to_right.at[i], left_sum.at[i], right_send.at[i], left_recv.at[i], some
                ).wait_recv()
                sum_right(i)
            i = 2 * n - 1 - z - step
            if z < n - 1 and 0 <= i < n:
                copy(
                    to_left.at[i], right_sum.at[i], left_send.at[i], right_recv.at[i], some
                ).wait_recv()
                sum_left(i)
            for i in range(n):
                from_left = z + 1 + i if z > 0 else 0
                from_right = 2 * n - 1 - z - i if z < n - 1 else 0
                if max(from_left, from_right) == step:
                    start_code(i)
                    waiting_code.append(i)
        for i in waiting_code:
            finish_code(i)
        for descriptor in sent:
            descriptor.wait_send()

    for z in range(n):
        pl.when(place == z)(functools.partial(program, z))


def exchange(n, nw, acts, dec_bias, enc_weight, enc_bias, dec_weight):
    rows, width = acts.shape
    latents = enc_weight.shape[1]
    wide = (n, rows, width)
    narrow = (n, rows, latents)
    parts = (nw,) + narrow
    dma = pltpu.SemaphoreType.DMA
    vmem = pl.BlockSpec(memory_space=pltpu.VMEM)
    return pl.pallas_call(
        functools.partial(exchange_kernel, n, nw),
        out_shape=[
            jax.ShapeDtypeStruct(wide, jnp.bfloat16),
            jax.ShapeDtypeStruct(narrow, jnp.bfloat16),
            jax.ShapeDtypeStruct(wide, jnp.bfloat16),
            jax.ShapeDtypeStruct(narrow, jnp.bfloat16),
        ],
        in_specs=[vmem] * 5,
        out_specs=[vmem] * 4,
        scratch_shapes=[
            pltpu.VMEM(wide, jnp.bfloat16),
            pltpu.VMEM(parts, jnp.float32),
            pltpu.VMEM(parts, jnp.float32),
            pltpu.VMEM(narrow, jnp.float32),
            pltpu.VMEM(wide, jnp.float32),
            pltpu.VMEM(wide, jnp.float32),
            pltpu.VMEM(wide, jnp.float32),
            pltpu.VMEM(wide, jnp.float32),
            pltpu.VMEM(wide, jnp.float32),
            pltpu.VMEM(wide, jnp.float32),
        ]
        + [dma((n,))] * 7
        + [dma((nw, n))] * 4,
        compiler_params=pltpu.CompilerParams(
            collective_id=0, has_side_effects=True, vmem_limit_bytes=32 * 2**20
        ),
        name="exchange",
    )(acts, dec_bias[None, :], enc_weight, enc_bias[None, :], dec_weight)


def update_kernel(
    centered,
    codes,
    grad_out,
    pre_grad,
    enc_m,
    enc_v,
    dec_m,
    dec_v,
    bias_m,
    bias_v,
    enc_moment,
    enc_second,
    enc_step,
    dec_moment,
    dec_second,
    dec_step,
    bias_moment,
    bias_second,
    bias_step,
):
    dec_grad = inner_rows(codes[...], grad_out[...])
    dec_moment[...], dec_second[...], dec_step[...] = adam_update(dec_m[...], dec_v[...], dec_grad)
    enc_grad = inner_rows(centered[...], pre_grad[...])
    enc_moment[...], enc_second[...], enc_step[...] = adam_update(enc_m[...], enc_v[...], enc_grad)

    @pl.when(pl.program_id(0) == 0)
    def _():
        bias_grad = jnp.sum(pre_grad[...].astype(jnp.float32), axis=0, keepdims=True)
        bias_moment[...], bias_second[...], bias_step[...] = adam_update(
            bias_m[...], bias_v[...], bias_grad
        )


def update(centered, codes, grad_out, pre_grad, enc_m, enc_v, dec_m, dec_v, bias_m, bias_v):
    rows, width = centered.shape
    latents = codes.shape[1]
    tile = 256 if width % 256 == 0 else width
    slab = pl.BlockSpec((rows, tile), lambda j: (0, j))
    whole = pl.BlockSpec((rows, latents), lambda j: (0, 0))
    enc = pl.BlockSpec((tile, latents), lambda j: (j, 0))
    dec = pl.BlockSpec((latents, tile), lambda j: (0, j))
    bias = pl.BlockSpec((1, latents), lambda j: (0, 0))

    def like(shape, dtype):
        return jax.ShapeDtypeStruct(shape, dtype)

    kinds = (jnp.float32, jnp.float32, jnp.bfloat16)
    return pl.pallas_call(
        update_kernel,
        grid=(width // tile,),
        out_shape=[like((width, latents), kind) for kind in kinds]
        + [like((latents, width), kind) for kind in kinds]
        + [like((1, latents), kind) for kind in kinds],
        in_specs=[slab, whole, slab, whole, enc, enc, dec, dec, bias, bias],
        out_specs=[enc] * 3 + [dec] * 3 + [bias] * 3,
        compiler_params=pltpu.CompilerParams(vmem_limit_bytes=32 * 2**20),
        name="update",
    )(centered, codes, grad_out, pre_grad, enc_m, enc_v, dec_m, dec_v, bias_m, bias_v)


def local_small(
    acts, dec_bias, enc_weight, enc_bias, dec_weight, enc_m, enc_v, dec_m, dec_v, bias_m, bias_v
):
    n, nw = lax.axis_size("latent"), lax.axis_size("width")
    width, latents = acts.shape[1], enc_weight.shape[1]
    centered, codes, grad_out, pre_grad = exchange(
        n, nw, acts, dec_bias, enc_weight, enc_bias, dec_weight
    )
    results = update(
        centered.reshape(-1, width),
        codes.reshape(-1, latents),
        grad_out.reshape(-1, width),
        pre_grad.reshape(-1, latents),
        enc_m,
        enc_v,
        dec_m,
        dec_v,
        bias_m[None, :],
        bias_v[None, :],
    )
    return (*results[:6], *(one.reshape(-1) for one in results[6:]))


def solution(mesh):
    in_specs = (
        P(("groups", "latent"), "width"),
        P(("groups", "width")),
        P("width", ("groups", "latent")),
        P(("groups", "latent")),
        P(("groups", "latent"), "width"),
        P("width", ("groups", "latent")),
        P("width", ("groups", "latent")),
        P(("groups", "latent"), "width"),
        P(("groups", "latent"), "width"),
        P(("groups", "latent")),
        P(("groups", "latent")),
    )
    out_specs = (
        P("width", ("groups", "latent")),
        P("width", ("groups", "latent")),
        P("width", ("groups", "latent")),
        P(("groups", "latent"), "width"),
        P(("groups", "latent"), "width"),
        P(("groups", "latent"), "width"),
        P(("groups", "latent")),
        P(("groups", "latent")),
        P(("groups", "latent")),
    )
    local = local_small if mesh.shape["latent"] <= 4 else local_large
    return jax.shard_map(local, mesh=mesh, in_specs=in_specs, out_specs=out_specs, check_vma=False)
```

```python
import functools

import jax
import jax.numpy as jnp
from jax import lax
from jax.experimental import pallas as pl
from jax.experimental.pallas import tpu as pltpu
from jax.sharding import PartitionSpec as P

ADAM_STEP = 10


BETA_ONE = 0.9
BETA_TWO = 0.95
EPSILON = 1e-08
SPARSITY = 0.5
SHARPNESS = 4.0

MESH = pl.DeviceIdType.MESH


def adam_update(moment, second, grad):
    moment_new = BETA_ONE * moment + (1.0 - BETA_ONE) * grad
    second_new = BETA_TWO * second + (1.0 - BETA_TWO) * grad * grad
    update_step = (
        moment_new
        / (1.0 - BETA_ONE**ADAM_STEP)
        / (jnp.sqrt(second_new / (1.0 - BETA_TWO**ADAM_STEP)) + EPSILON)
    )
    return (moment_new, second_new, update_step.astype(jnp.bfloat16))


def inner_rows(left, right):
    return lax.dot_general(
        left, right, (((0,), (0,)), ((), ())), preferred_element_type=jnp.float32
    )


def inner_cols(left, right):
    return lax.dot_general(
        left, right, (((1,), (1,)), ((), ())), preferred_element_type=jnp.float32
    )


def local_large(
    acts, dec_bias, enc_weight, enc_bias, dec_weight, enc_m, enc_v, dec_m, dec_v, bias_m, bias_v
):
    lat_groups = lax.axis_size("latent")
    rows_local = acts.shape[0]
    rows_all = rows_local * lat_groups
    incoming = lax.all_gather(acts, "latent", axis=0, tiled=True)
    centered_block = (incoming.astype(jnp.float32) - dec_bias).astype(jnp.bfloat16)
    product = jnp.dot(centered_block, enc_weight, preferred_element_type=jnp.float32)
    pre_part = product
    raw_rows = incoming
    centered = centered_block
    pre_part, raw_rows, centered = (pre_part, raw_rows, centered)
    pre = lax.psum(pre_part, "width") + enc_bias
    latent_code = (jax.nn.softplus(SHARPNESS * pre) / SHARPNESS).astype(jnp.bfloat16)
    codes = latent_code
    rebuilt = (
        lax.psum_scatter(
            jnp.dot(codes, dec_weight, preferred_element_type=jnp.float32),
            "latent",
            scatter_dimension=0,
            tiled=True,
        )
        + dec_bias
    )
    grad_out = (2.0 / rows_all * (rebuilt - acts.astype(jnp.float32))).astype(jnp.bfloat16)
    incoming = lax.all_gather(grad_out, "latent", axis=0, tiled=True)
    codes = latent_code
    dec_grad = inner_rows(codes, incoming)
    code_part = inner_cols(incoming, dec_weight)
    dec_grad, code_part = (dec_grad, code_part)
    code_grad = lax.psum(code_part, "width") + SPARSITY / rows_all
    pre_grad = (code_grad * jax.nn.sigmoid(SHARPNESS * pre)).astype(jnp.bfloat16)
    enc_grad = inner_rows(centered, pre_grad)
    bias_grad = jnp.sum(pre_grad.astype(jnp.float32), axis=0)
    enc_moment, enc_second, enc_step = adam_update(enc_m, enc_v, enc_grad)
    dec_moment, dec_second, dec_step = adam_update(dec_m, dec_v, dec_grad)
    bias_moment, bias_second, bias_step = adam_update(bias_m, bias_v, bias_grad)
    return (
        enc_moment,
        enc_second,
        enc_step,
        dec_moment,
        dec_second,
        dec_step,
        bias_moment,
        bias_second,
        bias_step,
    )


def exchange_kernel(
    n,
    nw,
    acts_ref,
    dec_bias_ref,
    enc_weight_ref,
    enc_bias_ref,
    dec_weight_ref,
    centered,
    codes,
    grad_out,
    pre_grad,
    acts_all,
    pre_parts,
    code_parts,
    slope,
    dec_all,
    codes_all,
    acts_recv,
    acts_send_right,
    acts_send_left,
    dec_recv,
    dec_send,
    codes_recv,
    codes_send,
    grad_recv,
    grad_send,
    pre_recv,
    pre_send,
    code_recv,
    code_send,
):
    place = lax.axis_index("latent")
    mine = lax.axis_index("width")
    rows_all = n * acts_ref.shape[0]
    half = acts_ref.shape[1] // 2
    peers = [lax.rem(mine + k, nw) for k in range(1, nw)]

    barrier = pltpu.get_barrier_semaphore()
    for peer in peers:
        pl.semaphore_signal(barrier, inc=1, device_id={"width": peer}, device_id_type=MESH)

    @pl.when(place > 0)
    def _():
        pl.semaphore_signal(barrier, inc=1, device_id={"latent": place - 1}, device_id_type=MESH)

    @pl.when(place < n - 1)
    def _():
        pl.semaphore_signal(barrier, inc=1, device_id={"latent": place + 1}, device_id_type=MESH)

    pl.semaphore_wait(
        barrier, nw - 1 + jnp.where(place > 0, 1, 0) + jnp.where(place < n - 1, 1, 0)
    )

    def program(z):
        sent = []
        right = {"latent": place + 1}
        left = {"latent": place - 1}
        inward = right if z < n // 2 else left
        outward = left if z < n // 2 else right

        def columns(h):
            return pl.ds(h * half, half)

        def acts_block(b):
            return acts_ref if b == z else acts_all.at[b]

        def copy(src, dst, send, recv, where):
            return pltpu.make_async_remote_copy(
                src_ref=src,
                dst_ref=dst,
                send_sem=send,
                recv_sem=recv,
                device_id=where,
                device_id_type=MESH,
            )

        def send(*arguments):
            descriptor = copy(*arguments)
            descriptor.start()
            sent.append(descriptor)

        def acts_right(b):
            send(acts_block(b), acts_all.at[b], acts_send_right.at[b], acts_recv.at[b], right)

        def acts_left(b):
            send(acts_block(b), acts_all.at[b], acts_send_left.at[b], acts_recv.at[b], left)

        def to_peers(parts, b, send_sem, recv_sem):
            for k in range(1, nw):
                block = parts.at[mine, b]
                send(block, block, send_sem.at[k, b], recv_sem.at[k, b], {"width": peers[k - 1]})

        def from_peers(parts, b, send_sem, recv_sem):
            for k in range(1, nw):
                block = parts.at[mine, b]
                copy(
                    block, block, send_sem.at[k, b], recv_sem.at[k, b], {"width": peers[k - 1]}
                ).wait_recv()
            total = parts[0, b]
            for other in range(1, nw):
                total = total + parts[other, b]
            return total

        def start_pre(b):
            rounded = (acts_block(b)[...].astype(jnp.float32) - dec_bias_ref[...]).astype(
                jnp.bfloat16
            )
            centered[b] = rounded
            pre_parts[mine, b] = jnp.dot(
                rounded, enc_weight_ref[...], preferred_element_type=jnp.float32
            )
            to_peers(pre_parts, b, pre_send, pre_recv)

        def finish_pre(b):
            scaled = SHARPNESS * (from_peers(pre_parts, b, pre_send, pre_recv) + enc_bias_ref[...])
            small = jnp.exp(-jnp.abs(scaled))
            code = ((jnp.maximum(scaled, 0.0) + jnp.log1p(small)) / SHARPNESS).astype(jnp.bfloat16)
            slope[b] = jnp.where(scaled >= 0, 1.0, small) / (1.0 + small)
            codes[b] = code
            send_codes(z, b)

        def codes_block(k, b):
            return codes.at[b] if k == z else codes_all.at[k, b]

        def send_codes(k, b):
            send(
                codes_block(k, b),
                codes_all.at[k, b],
                codes_send.at[k, b],
                codes_recv.at[k, b],
                inward,
            )

        def wait_codes(k, b):
            block = codes_all.at[k, b]
            copy(block, block, codes_send.at[k, b], codes_recv.at[k, b], inward).wait_recv()

        def dec_block(k, h):
            return dec_weight_ref.at[:, columns(h)] if k == z else dec_all.at[k, h]

        def send_dec(k, h):
            send(
                dec_block(k, h), dec_all.at[k, h], dec_send.at[k, h], dec_recv.at[k, h], inward
            )

        def wait_dec(k, h):
            block = dec_all.at[k, h]
            copy(block, block, dec_send.at[k, h], dec_recv.at[k, h], inward).wait_recv()

        def make_grad(h, i):
            rebuilt = dec_bias_ref[:, columns(h)]
            for k in range(n):
                rebuilt = rebuilt + jnp.dot(
                    codes_block(k, i)[...],
                    dec_block(k, h)[...],
                    preferred_element_type=jnp.float32,
                )
            raw = acts_block(i)[:, columns(h)].astype(jnp.float32)
            grad_out[i, :, columns(h)] = (2.0 / rows_all * (rebuilt - raw)).astype(jnp.bfloat16)
            block = grad_out.at[i, :, columns(h)]
            send(block, block, grad_send.at[h, i], grad_recv.at[h, i], outward)

        def wait_grad(h, i):
            block = grad_out.at[i, :, columns(h)]
            copy(block, block, grad_send.at[h, i], grad_recv.at[h, i], inward).wait_recv()

        def start_code(i):
            code_parts[mine, i] = inner_cols(grad_out[i], dec_weight_ref[...])
            to_peers(code_parts, i, code_send, code_recv)

        def finish_code(i):
            code_grad = from_peers(code_parts, i, code_send, code_recv) + SPARSITY / rows_all
            pre_grad[i] = (code_grad * slope[i]).astype(jnp.bfloat16)

        def wait_acts(b):
            block = acts_all.at[b]
            copy(block, block, acts_send_right.at[b], acts_recv.at[b], inward).wait_recv()

        if z in (0, 3):
            order = [0, 1, 2, 3] if z == 0 else [3, 2, 1, 0]
            (acts_right if z == 0 else acts_left)(z)
            start_pre(z)
            send_dec(z, 0)
            send_dec(z, 1)
            for before, b in zip(order, order[1:]):
                finish_pre(before)
                wait_acts(b)
                start_pre(b)
            finish_pre(order[3])
            for i in range(n):
                wait_grad(0, i)
            for i in range(n):
                wait_grad(1, i)
                start_code(i)
                if i > 0:
                    finish_code(i - 1)
            finish_code(n - 1)
        else:
            end, middle, far = (0, 2, 3) if z == 1 else (3, 1, 0)
            to_end, to_middle = (acts_left, acts_right) if z == 1 else (acts_right, acts_left)
            to_middle(z)
            to_end(z)
            start_pre(z)
            finish_pre(z)
            wait_acts(end)
            to_middle(end)
            wait_acts(middle)
            to_end(middle)
            start_pre(end)
            start_pre(middle)
            send_dec(z, 0)
            finish_pre(end)
            finish_pre(middle)
            wait_dec(end, 0)
            send_dec(end, 0)
            wait_acts(far)
            to_end(far)
            start_pre(far)
            send_dec(z, 1)
            for b in (end, z):
                wait_codes(end, b)
                send_codes(end, b)
            finish_pre(far)
            wait_dec(end, 1)
            send_dec(end, 1)
            for b in (middle, far):
                wait_codes(end, b)
                send_codes(end, b)
            for k in (middle, far):
                for b in range(n):
                    wait_codes(k, b)
                wait_dec(k, 0)
            for i in range(n):
                make_grad(0, i)
            for k in (middle, far):
                wait_dec(k, 1)
            for i in range(n):
                make_grad(1, i)
                start_code(i)
            for i in range(n):
                finish_code(i)
        for descriptor in sent:
            descriptor.wait_send()

    for z in range(n):
        pl.when(place == z)(functools.partial(program, z))


def exchange(n, nw, acts, dec_bias, enc_weight, enc_bias, dec_weight):
    rows, width = acts.shape
    latents = enc_weight.shape[1]
    wide = (n, rows, width)
    narrow = (n, rows, latents)
    parts = (nw,) + narrow
    dma = pltpu.SemaphoreType.DMA
    vmem = pl.BlockSpec(memory_space=pltpu.VMEM)
    return pl.pallas_call(
        functools.partial(exchange_kernel, n, nw),
        out_shape=[
            jax.ShapeDtypeStruct(wide, jnp.bfloat16),
            jax.ShapeDtypeStruct(narrow, jnp.bfloat16),
            jax.ShapeDtypeStruct(wide, jnp.bfloat16),
            jax.ShapeDtypeStruct(narrow, jnp.bfloat16),
        ],
        in_specs=[vmem] * 5,
        out_specs=[vmem] * 4,
        scratch_shapes=[
            pltpu.VMEM(wide, jnp.bfloat16),
            pltpu.VMEM(parts, jnp.float32),
            pltpu.VMEM(parts, jnp.float32),
            pltpu.VMEM(narrow, jnp.float32),
            pltpu.VMEM((n, 2, latents, width // 2), jnp.bfloat16),
            pltpu.VMEM((n, n, rows, latents), jnp.bfloat16),
            dma((n,)),
            dma((n,)),
            dma((n,)),
            dma((n, 2)),
            dma((n, 2)),
            dma((n, n)),
            dma((n, n)),
            dma((2, n)),
            dma((2, n)),
        ]
        + [dma((nw, n))] * 4,
        compiler_params=pltpu.CompilerParams(
            collective_id=0, has_side_effects=True, vmem_limit_bytes=56 * 2**20
        ),
        name="exchange",
    )(acts, dec_bias[None, :], enc_weight, enc_bias[None, :], dec_weight)


def update_kernel(
    centered,
    codes,
    grad_out,
    pre_grad,
    enc_m,
    enc_v,
    dec_m,
    dec_v,
    bias_m,
    bias_v,
    enc_moment,
    enc_second,
    enc_step,
    dec_moment,
    dec_second,
    dec_step,
    bias_moment,
    bias_second,
    bias_step,
):
    dec_grad = inner_rows(codes[...], grad_out[...])
    dec_moment[...], dec_second[...], dec_step[...] = adam_update(dec_m[...], dec_v[...], dec_grad)
    enc_grad = inner_rows(centered[...], pre_grad[...])
    enc_moment[...], enc_second[...], enc_step[...] = adam_update(enc_m[...], enc_v[...], enc_grad)

    @pl.when(pl.program_id(0) == 0)
    def _():
        bias_grad = jnp.sum(pre_grad[...].astype(jnp.float32), axis=0, keepdims=True)
        bias_moment[...], bias_second[...], bias_step[...] = adam_update(
            bias_m[...], bias_v[...], bias_grad
        )


def update(centered, codes, grad_out, pre_grad, enc_m, enc_v, dec_m, dec_v, bias_m, bias_v):
    rows, width = centered.shape
    latents = codes.shape[1]
    tile = 256 if width % 256 == 0 else width
    slab = pl.BlockSpec((rows, tile), lambda j: (0, j))
    whole = pl.BlockSpec((rows, latents), lambda j: (0, 0))
    enc = pl.BlockSpec((tile, latents), lambda j: (j, 0))
    dec = pl.BlockSpec((latents, tile), lambda j: (0, j))
    bias = pl.BlockSpec((1, latents), lambda j: (0, 0))

    def like(shape, dtype):
        return jax.ShapeDtypeStruct(shape, dtype)

    kinds = (jnp.float32, jnp.float32, jnp.bfloat16)
    return pl.pallas_call(
        update_kernel,
        grid=(width // tile,),
        out_shape=[like((width, latents), kind) for kind in kinds]
        + [like((latents, width), kind) for kind in kinds]
        + [like((1, latents), kind) for kind in kinds],
        in_specs=[slab, whole, slab, whole, enc, enc, dec, dec, bias, bias],
        out_specs=[enc] * 3 + [dec] * 3 + [bias] * 3,
        compiler_params=pltpu.CompilerParams(vmem_limit_bytes=56 * 2**20),
        name="update",
    )(centered, codes, grad_out, pre_grad, enc_m, enc_v, dec_m, dec_v, bias_m, bias_v)


def local_small(
    acts, dec_bias, enc_weight, enc_bias, dec_weight, enc_m, enc_v, dec_m, dec_v, bias_m, bias_v
):
    n, nw = lax.axis_size("latent"), lax.axis_size("width")
    width, latents = acts.shape[1], enc_weight.shape[1]
    centered, codes, grad_out, pre_grad = exchange(
        n, nw, acts, dec_bias, enc_weight, enc_bias, dec_weight
    )
    results = update(
        centered.reshape(-1, width),
        codes.reshape(-1, latents),
        grad_out.reshape(-1, width),
        pre_grad.reshape(-1, latents),
        enc_m,
        enc_v,
        dec_m,
        dec_v,
        bias_m[None, :],
        bias_v[None, :],
    )
    return (*results[:6], *(one.reshape(-1) for one in results[6:]))


def solution(mesh):
    in_specs = (
        P(("groups", "latent"), "width"),
        P(("groups", "width")),
        P("width", ("groups", "latent")),
        P(("groups", "latent")),
        P(("groups", "latent"), "width"),
        P("width", ("groups", "latent")),
        P("width", ("groups", "latent")),
        P(("groups", "latent"), "width"),
        P(("groups", "latent"), "width"),
        P(("groups", "latent")),
        P(("groups", "latent")),
    )
    out_specs = (
        P("width", ("groups", "latent")),
        P("width", ("groups", "latent")),
        P("width", ("groups", "latent")),
        P(("groups", "latent"), "width"),
        P(("groups", "latent"), "width"),
        P(("groups", "latent"), "width"),
        P(("groups", "latent")),
        P(("groups", "latent")),
        P(("groups", "latent")),
    )
    local = local_small if mesh.shape["latent"] == 4 else local_large
    return jax.shard_map(local, mesh=mesh, in_specs=in_specs, out_specs=out_specs, check_vma=False)
```
